32 devices in a mesh: grp: 2 (over y), row: 16 (over z, x, core).
Axes of the slice: x: 2, y: 2, z: 4, core: 2. Of those that a mesh axis runs over, the one named last changes fastest.
Arguments:
- features: bfloat16 [16384, 256], P(('grp', 'row')), may hold values from -6 to 6
- weight: bfloat16 [256, 256], replicated, may hold values from -0.375 to 0.375
- block_vals: bfloat16 [2, 128, 16, 128, 128], P('grp', 'row'), may hold values from -0.125 to 0.125
- block_cols: int32 [2, 128, 16], P('grp', 'row'), may hold values from 0 to 63, as said below
- block_count: int32 [2, 128], P('grp', 'row'), may hold values from 1 to 16, as said below
- cotangent: bfloat16 [16384, 256], P(('grp', 'row')), may hold values from -6 to 6
Outputs:
- activated: bfloat16 [16384, 256], P(('grp', 'row'))
- weight_grad: float32 [256, 256], replicated
- input_grad: bfloat16 [16384, 256], P(('grp', 'row'))
The draws below stay inside these ranges and needn't reach their ends.
Inputs may be any that keep to these rules, and one draw needn't show every extreme that they name: `block_cols`: within one destination row block the 16 column blocks are distinct and ascending. `block_count`: in every draw some device holds 16 live slots in each of its row blocks.
All inputs are finite; a program needn't handle non-finite values.
Results may differ from the reference program's by a relative error of at most 0.0062.
Values may be sent and summed in bfloat16 or wider, within the bound.
A program may use at most 128 MiB of HBM per device.

```python
import math
import jax
import jax.numpy as jnp
from jax import lax

F = 256
BS = 128
KR = 16
V_DEV = 512
VERTS = 16384
RB_DEV = 8
ROWBLK = 128
PCB = 64
N_GRP = 2
N_ROW = 16


def draw_block_cols(key, part):
    scores = jax.random.randint(key, (N_GRP, ROWBLK, PCB), 0, 1 << 20)
    scores = scores * PCB + jnp.arange(PCB, dtype=jnp.int32)[None, None, :]
    order = jnp.argsort(scores, axis=-1)[:, :, :KR]
    return jnp.sort(order, axis=-1).astype(jnp.int32)


def draw_block_count(key, part):
    first, second, third = jax.random.split(jax.random.fold_in(key, 17), 3)
    shifts = jax.random.randint(first, (N_GRP, N_ROW, 1), 0, 4)
    levels = jax.random.randint(second, (N_GRP, N_ROW, RB_DEV), 12, 17)
    counts = jnp.right_shift(KR * levels // 16, shifts)
    counts = jnp.maximum(counts, 1)
    busiest = jax.random.randint(third, (), 0, N_GRP * N_ROW)
    device_ids = jnp.arange(N_GRP * N_ROW, dtype=jnp.int32).reshape(N_GRP, N_ROW, 1)
    counts = jnp.where(device_ids == busiest, KR, counts)
    return counts.reshape(N_GRP, N_ROW * RB_DEV).astype(jnp.int32)


def steps_of(stream_key, shape, shards, low, high):
    loudness, own = 1.0, jax.random.fold_in(stream_key, 6)
    for position, blocks in shards:
        draws = jnp.exp(jax.random.uniform(jax.random.fold_in(own, position), (blocks,), jnp.float32, low / len(shards), high / len(shards)))
        loudness = loudness * jnp.repeat(draws, shape[position] // blocks).reshape([-1 if axis == position else 1 for axis in range(len(shape))])
    return loudness


def bell_draw(stream_key, dims, scale, reach, shards=(), held_as=jnp.bfloat16):
    factor_of = steps_of(stream_key, dims, shards, -0.22, 0.18) if shards else 1.0
    result = jax.random.normal(stream_key, dims, jnp.float32) * scale * factor_of
    return jnp.minimum(jnp.maximum(result, -reach), reach).astype(held_as)


def setup_inputs(seed: int = 0) -> dict:
    streams_of = jax.random.split(jax.random.key(seed), 7)
    features = bell_draw(streams_of[0], (VERTS, F), 1.0, 6.0, ((0, 32),))
    weight = bell_draw(streams_of[1], (F, F), F ** -0.5, 0.375)
    block_vals = bell_draw(streams_of[2], (N_GRP, ROWBLK, KR, BS, BS), (KR * BS) ** -0.5, 0.125, ((0, 2), (1, 16)))
    block_cols = draw_block_cols(jax.random.fold_in(streams_of[6], 71), 0)
    block_count = draw_block_count(jax.random.fold_in(streams_of[6], 71), 0)
    cotangent = bell_draw(streams_of[5], (VERTS, F), 1.0, 6.0, ((0, 32),))
    return {"features": features, "weight": weight, "block_vals": block_vals, "block_cols": block_cols, "block_count": block_count, "cotangent": cotangent}


def silu_slope(pre):
    sigma = jax.nn.sigmoid(pre)
    return sigma * (1.0 + pre * (1.0 - sigma))

def reference(features, weight, block_vals, block_cols, block_count, cotangent):
    slots = jnp.arange(KR)
    panel_rows = N_ROW * V_DEV
    per_dev = V_DEV // BS
    partial_total = jnp.zeros((VERTS, F), jnp.float32)
    for group in range(N_GRP):
        panel_blocks = features[group * panel_rows:(group + 1) * panel_rows].reshape(PCB, BS, F)

        def aggregate(items):
            values, columns, count = items
            masked = jnp.where((slots < count)[:, None, None], values, jnp.zeros_like(values))
            picked = panel_blocks[columns]
            return jnp.einsum('kij,kjf->if', masked.astype(jnp.float32), picked.astype(jnp.float32))
        sums = lax.map(aggregate, (block_vals[group], block_cols[group], block_count[group]))
        sums = sums.reshape(N_ROW, N_GRP, per_dev, BS, F).transpose(1, 0, 2, 3, 4).reshape(VERTS, F)
        partial_total = partial_total + sums
    aggregated = partial_total.astype(jnp.bfloat16)
    pre = jnp.dot(aggregated, weight, preferred_element_type=jnp.float32)
    activated = jax.nn.silu(pre).astype(jnp.bfloat16)
    pre_grad = (cotangent.astype(jnp.float32) * silu_slope(pre)).astype(jnp.bfloat16)
    weight_grad = jnp.dot(aggregated.T, pre_grad, preferred_element_type=jnp.float32) * (1.0 / math.sqrt(VERTS))
    agg_grad = jnp.dot(pre_grad, weight.T, preferred_element_type=jnp.float32).astype(jnp.bfloat16)
    by_block = agg_grad.reshape(N_GRP, N_ROW, per_dev, BS, F).transpose(1, 0, 2, 3, 4).reshape(ROWBLK, BS, F)
    panels = []
    for group in range(N_GRP):

        def spread(carry, items):
            values, columns, count, grad_rows = items
            masked = jnp.where((slots < count)[:, None, None], values, jnp.zeros_like(values))
            contrib = jnp.einsum('kij,if->kjf', masked.astype(jnp.float32), grad_rows.astype(jnp.float32))
            return (carry.at[columns].add(contrib), None)
        total, unused = lax.scan(spread, jnp.zeros((PCB, BS, F), jnp.float32), (block_vals[group], block_cols[group], block_count[group], by_block))
        panels.append(total.reshape(PCB * BS, F))
    input_grad = jnp.concatenate(panels, axis=0).astype(jnp.bfloat16)
    return (activated, weight_grad, input_grad)
```

```python
import functools
import math

import jax
import jax.numpy as jnp
from jax import lax
from jax.experimental import pallas as pl
from jax.experimental.pallas import tpu as pltpu
from jax.sharding import PartitionSpec as P

MESH = pl.DeviceIdType.MESH
F32 = jnp.float32
BF16 = jnp.bfloat16
BS = 128
VD = 512
TB = 8
CW, CCW = 0, 1


def dot(a, b):
    return jnp.dot(a, b, preferred_element_type=F32)


def kernel(
    n, keep, scale,
    inv_ref, feat_ref, w_ref, vals_hbm, cot_ref,
    act_ref, wg_ref, ig_ref,
    panel, vals, dense, acc, ys, yr, agg, pgr, gt, part, sibp, fresh, rsr,
    wl, w1, s1, w2, wp, w3, w4, wo,
    vals_sem, ag_s, ag_r, sb_s, sb_r, so_s, so_r, y_s, y_r, g_s, g_r,
    sp_s, sp_r, rs_s, rs_r, wa_s, wa_r, wb_s, wb_r, wc_s, wc_r, wd_s, wd_r, we_s, we_r,
):
    half = n // 2
    slots = vals.shape[1] - 1
    cols = n * TB
    grp = lax.axis_index("grp")
    row = lax.axis_index("row")
    core = lax.rem(row, 2)
    q = lax.div(row, 2)
    odd = lax.rem(q, 2)
    p = (1 - odd) * lax.div(q, 2) + odd * (n - lax.div(q + 1, 2))

    def chip(offset):
        at = lax.rem(p + offset + n, n)
        back = lax.div(at, half)
        return (1 - back) * 2 * at + back * (2 * (n - at) - 1)

    def peer(chip_id):
        return (grp, chip_id * 2 + core)

    sibling = (grp, q * 2 + 1 - core)
    partner = (1 - grp, row)
    across = (1 - grp, q * 2 + 1 - core)

    def rcopy(src, dst, ss, rs, dev):
        return pltpu.make_async_remote_copy(
            src_ref=src, dst_ref=dst, send_sem=ss, recv_sem=rs,
            device_id=dev, device_id_type=MESH,
        )

    load = pltpu.make_async_copy(vals_hbm, vals.at[:, pl.ds(0, slots)], vals_sem)
    load.start()

    barrier = pltpu.get_barrier_semaphore()
    for dev in [peer(chip(o)) for o in range(1, n)] + [sibling, partner, across]:
        pl.semaphore_signal(barrier, inc=1, device_id=dev, device_id_type=MESH)
    for h in range(2):
        panel[q, core * 2 + h] = feat_ref[pl.ds(h * 256, 256), :]
    for t in range(TB):
        vals[t, slots] = jnp.zeros((BS, BS), BF16)
    pl.semaphore_wait(barrier, n - 1 + 3)

    step = {CW: 1, CCW: -1}

    def lane(d, i):
        return i % 2 if d == CW else 1 - i % 2

    def ag(d, i):
        src = panel.at[chip(-step[d] * (i // 2)), core * 2 + lane(d, i)]
        return rcopy(src, src, ag_s.at[d, i], ag_r.at[d, i], peer(chip(step[d])))

    def ag_in(d, i):
        src = panel.at[chip(-step[d] * (i // 2 + 1)), core * 2 + lane(d, i)]
        return rcopy(src, src, ag_s.at[d, i], ag_r.at[d, i], peer(chip(step[d])))

    def sib(d, i, c):
        src = panel.at[chip(-step[d] * (i // 2 + 1)), c * 2 + lane(d, i)]
        return rcopy(src, src, sb_s.at[d, i], sb_r.at[d, i], sibling)

    def sib_own(c):
        src = panel.at[q, pl.ds(c * 2, 2)]
        return rcopy(src, src, so_s, so_r, sibling)

    def where_dense(chip_id):
        return chip_id if keep else 0

    def build(chip_id):
        to = where_dense(chip_id)

        def rows(t, carry):
            for j in range(TB):
                k = inv_ref[t * cols + chip_id * TB + j]
                dense[to, pl.ds(t * BS, BS), pl.ds(j * BS, BS)] = vals[t, k]
            return carry

        lax.fori_loop(0, TB, rows, 0)

    def forward(chip_id, first=False):
        build(chip_id)
        to = where_dense(chip_id)

        def rows(m, carry):
            at = pl.ds(pl.multiple_of(m * 256, 256), 256)
            v = dot(dense[to, at, :], panel[chip_id].reshape(4 * 256, 256))
            acc[at, :] = v if first else acc[at, :] + v
            return carry

        lax.fori_loop(0, 4, rows, 0)

    for i in range(2):
        for d in (CW, CCW):
            ag(d, i).start()
    sib_own(core).start()
    load.wait()

    def arrive(i):
        for d in (CW, CCW):
            ag_in(d, i).wait_recv()
            if i + 2 < n - 1:
                ag(d, i + 2).start()
            sib(d, i, core).start()

    def sib_wait(dist, d):
        for i in (2 * dist - 2, 2 * dist - 1):
            sib(d, i, 1 - core).wait_recv()

    sib_own(1 - core).wait_recv()
    forward(q, True)
    for dist in range(1, half):
        arrive(2 * dist - 2)
        if dist > 1:
            sib_wait(dist - 1, CW)
            forward(chip(-(dist - 1)))
        arrive(2 * dist - 1)
        if dist > 1:
            sib_wait(dist - 1, CCW)
            forward(chip(dist - 1))
    for d in (CW, CCW):
        sib_wait(half - 1, d)
        forward(chip(-step[d] * (half - 1)))
    far = chip(half)
    build(far)
    arrive(n - 2)
    for d in (CW, CCW):
        sib(d, n - 2, 1 - core).wait_recv()

    at_far = where_dense(far)
    mine, theirs = grp * VD, (1 - grp) * VD

    def yc(k):
        return rcopy(ys.at[k], yr.at[k], y_s.at[k], y_r.at[k], partner)

    for k in range(4):
        at = pl.ds(pl.multiple_of(theirs + k * BS, BS), BS)
        v = acc[at, :] + dot(dense[at_far, at, :], panel[far].reshape(4 * 256, 256))
        ys[k] = v.astype(BF16)
        yc(k).start()
    for k in range(2):
        at = pl.ds(pl.multiple_of(mine + k * 256, 256), 256)
        acc[at, :] += dot(dense[at_far, at, :], panel[far].reshape(4 * 256, 256))

    def gc(k, base):
        ref = gt.at[:, pl.ds(pl.multiple_of(base + k * BS, BS), BS)]
        return rcopy(ref, ref, g_s.at[k], g_r.at[k], partner)

    for k in range(4):
        yc(k).wait_recv()
        here = pl.ds(k * BS, BS)
        at = pl.ds(pl.multiple_of(mine + k * BS, BS), BS)
        a = (acc[at, :] + yr[k].astype(F32)).astype(BF16)
        agg[here, :] = a
        pre = dot(a, w_ref[...])
        s = jax.nn.sigmoid(pre)
        act_ref[here, :] = (pre * s).astype(BF16)
        grad = (cot_ref[here, :].astype(F32) * (s * (1.0 + pre * (1.0 - s)))).astype(BF16)
        pgr[here, :] = grad
        back = lax.dot_general(
            w_ref[...], grad, (((1,), (1,)), ((), ())), preferred_element_type=F32
        )
        gt[:, at] = back.astype(BF16)
        gc(k, mine).start()
    local = lax.dot_general(
        agg[...], pgr[...], (((0,), (0,)), ((), ())), preferred_element_type=F32
    )
    for c in range(2):
        wl[c] = local[c * 128 : (c + 1) * 128]

    wa = lambda: rcopy(wl.at[1 - core], w1, wa_s, wa_r, sibling)
    wb = lambda: rcopy(s1.at[1 - grp], w2, wb_s, wb_r, partner)
    wc = lambda o: rcopy(wp.at[chip(o)], w3.at[q], wc_s.at[o], wc_r.at[o], peer(chip(o)))
    wd = lambda o: rcopy(w4.at[q], w4.at[q], wd_s.at[o], wd_r.at[o], peer(chip(o)))
    me_wo = core * 2 + grp
    outs = (sibling, partner, across)
    theirs_wo = ((1 - core) * 2 + grp, core * 2 + 1 - grp, (1 - core) * 2 + 1 - grp)
    we = lambda k: rcopy(wo.at[me_wo], wo.at[me_wo], we_s.at[k], we_r.at[k], outs[k])
    share = 64 // n

    def w_stage1():
        wa().wait_recv()
        total = wl[core] + w1[...]
        for k in range(2):
            s1[k] = total[k * 64 : (k + 1) * 64]
        wb().start()

    def w_stage2():
        wb().wait_recv()
        total = s1[grp] + w2[...]
        for k in range(n):
            wp[k] = total[k * share : (k + 1) * share]
        for o in range(1, n):
            wc(o).start()
        w3[q] = wp[q]

    def w_stage3():
        for o in range(1, n):
            rcopy(wp.at[q], w3.at[chip(-o)], wc_s.at[o], wc_r.at[o], peer(chip(o))).wait_recv()
        total = w3[0]
        for k in range(1, n):
            total = total + w3[k]
        w4[q] = total * scale
        for o in range(1, n):
            wd(o).start()

    def w_stage4():
        for o in range(1, n):
            there = w4.at[chip(-o)]
            rcopy(there, there, wd_s.at[o], wd_r.at[o], peer(chip(o))).wait_recv()
        for k in range(n):
            wo[me_wo, pl.ds(k * share, share), :] = w4[k]
        for k in range(3):
            we(k).start()

    def w_stage5():
        for k in range(3):
            there = wo.at[theirs_wo[k]]
            rcopy(there, there, we_s.at[k], we_r.at[k], outs[k]).wait_recv()
        for k in range(4):
            wg_ref[pl.ds(k * 64, 64), :] = wo[k]

    wa().start()
    for k in range(4):
        gc(k, theirs).wait_recv()

    def backward(chip_id):
        if not keep:
            build(chip_id)
        to = where_dense(chip_id)
        for j in range(4):
            v = dot(gt[...], dense[to, :, pl.ds(j * 256, 256)])
            part[chip_id, j] = v.astype(BF16)
        sp(chip_id).start()

    def sp(chip_id):
        return rcopy(
            part.at[chip_id, pl.ds((1 - core) * 2, 2)], sibp.at[chip_id],
            sp_s.at[chip_id], sp_r.at[chip_id], sibling,
        )

    def rs(d, i):
        src = rsr.at[d, i + 2] if i + 2 < n - 1 else fresh.at[d, i - (n - 3)]
        return rcopy(src, rsr.at[d, i], rs_s.at[d, i], rs_r.at[d, i], peer(chip(-step[d])))

    def summed(d, i):
        chip_id = chip(-step[d] * (i // 2 + 1))
        h = lane(d, i)
        own = part[chip_id, core * 2 + h].astype(F32) + sibp[chip_id, h].astype(F32)
        if i + 2 < n - 1:
            rs(d, i + 2).wait_recv()
            rsr[d, i + 2] = (own + rsr[d, i + 2].astype(F32)).astype(BF16)
        else:
            fresh[d, i - (n - 3)] = own.astype(BF16)
        rs(d, i).start()

    backward(far)
    backward(chip(-(half - 1)))
    sp(far).wait_recv()
    for d in (CW, CCW):
        summed(d, n - 2)
    w_stage1()
    backward(chip(half - 1))
    stages = [w_stage2, w_stage3, w_stage4]
    for dist in range(half - 1, 0, -1):
        for d in (CW, CCW):
            sp(chip(-step[d] * dist)).wait_recv()
            summed(d, 2 * dist - 1)
        if dist > 1:
            backward(chip(-(dist - 1)))
            backward(chip(dist - 1))
        else:
            backward(q)
        if stages:
            stages.pop(0)()
        for d in (CW, CCW):
            summed(d, 2 * dist - 2)
    for stage in stages:
        stage()
    sp(q).wait_recv()
    for h in range(2):
        total = part[q, core * 2 + h].astype(F32) + sibp[q, h].astype(F32)
        for d in (CW, CCW):
            i = h if d == CW else 1 - h
            rs(d, i).wait_recv()
            total = total + rsr[d, i].astype(F32)
        ig_ref[pl.ds(h * 256, 256), :] = total.T.astype(BF16)
    w_stage5()

    for d in (CW, CCW):
        for i in range(n - 1):
            ag(d, i).wait_send()
            sib(d, i, core).wait_send()
            rs(d, i).wait_send()
    sib_own(core).wait_send()
    for k in range(4):
        yc(k).wait_send()
        gc(k, mine).wait_send()
    for k in range(n):
        sp(k).wait_send()
    wa().wait_send()
    wb().wait_send()
    for o in range(1, n):
        wc(o).wait_send()
        wd(o).wait_send()
    for k in range(3):
        we(k).wait_send()


def body(features, weight, block_vals, block_cols, block_count, cotangent):
    rows_dev, width = features.shape
    slots = block_vals.shape[2]
    groups = lax.axis_size("grp")
    members = lax.axis_size("row")
    verts = rows_dev * groups * members
    n = members // 2
    cols = members * rows_dev // BS
    keep = n <= 8
    live = jnp.arange(slots)[None, :] < block_count[0][:, None]
    hit = (block_cols[0][:, :, None] == jnp.arange(cols)[None, None, :]) & live[:, :, None]
    inv = slots + jnp.sum(
        jnp.where(hit, jnp.arange(slots)[None, :, None] - slots, 0), axis=1
    ).astype(jnp.int32)
    dma, vm = pltpu.SemaphoreType.DMA, pltpu.VMEM
    share = 64 // n
    scratch = [
        vm((n, 4, 256, width), BF16),
        vm((TB, slots + 1, BS, BS), BF16),
        vm((n if keep else 1, 1024, 1024), BF16),
        vm((1024, width), F32),
        vm((4, BS, width), BF16),
        vm((4, BS, width), BF16),
        vm((rows_dev, width), BF16),
        vm((rows_dev, width), BF16),
        vm((width, 1024), BF16),
        vm((n, 4, width, 256), BF16),
        vm((n, 2, width, 256), BF16),
        vm((2, 2, width, 256), BF16),
        vm((2, n - 1, width, 256), BF16),
        vm((2, 128, width), F32),
        vm((128, width), F32),
        vm((2, 64, width), F32),
        vm((64, width), F32),
        vm((n, share, width), F32),
        vm((n, share, width), F32),
        vm((n, share, width), F32),
        vm((4, 64, width), F32),
        dma,
        dma((2, n - 1)), dma((2, n - 1)),
        dma((2, n - 1)), dma((2, n - 1)),
        dma, dma,
        dma((4,)), dma((4,)), dma((4,)), dma((4,)),
        dma((n,)), dma((n,)),
        dma((2, n - 1)), dma((2, n - 1)),
        dma, dma, dma, dma,
        dma((n,)), dma((n,)), dma((n,)), dma((n,)),
        dma((3,)), dma((3,)),
    ]
    whole = pl.BlockSpec(memory_space=pltpu.VMEM)
    return pl.pallas_call(
        functools.partial(kernel, n, keep, 1.0 / math.sqrt(verts)),
        out_shape=(
            jax.ShapeDtypeStruct((rows_dev, width), BF16),
            jax.ShapeDtypeStruct((width, width), F32),
            jax.ShapeDtypeStruct((rows_dev, width), BF16),
        ),
        in_specs=[
            pl.BlockSpec(memory_space=pltpu.SMEM),
            whole,
            whole,
            pl.BlockSpec(memory_space=pl.ANY),
            whole,
        ],
        out_specs=(whole, whole, whole),
        scratch_shapes=scratch,
        compiler_params=pltpu.CompilerParams(
            collective_id=0, has_side_effects=True, vmem_limit_bytes=60 * 1024 * 1024
        ),
    )(inv.reshape(-1), features, weight, block_vals[0], cotangent)


def solution(mesh):
    placed = (
        P(("grp", "row"), None),
        P(),
        P("grp", "row", None, None, None),
        P("grp", "row", None),
        P("grp", "row"),
        P(("grp", "row"), None),
    )
    return jax.shard_map(
        body,
        mesh=mesh,
        in_specs=placed,
        out_specs=(P(("grp", "row"), None), P(), P(("grp", "row"), None)),
        check_vma=False,
    )
```

```python
import functools
import math

import jax
import jax.numpy as jnp
from jax import lax
from jax.experimental import pallas as pl
from jax.experimental.pallas import tpu as pltpu
from jax.sharding import PartitionSpec as P

MESH = pl.DeviceIdType.MESH
F32 = jnp.float32
BF16 = jnp.bfloat16
BS = 128
VD = 512
TB = 8
CW, CCW = 0, 1


def dot(a, b):
    return jnp.dot(a, b, preferred_element_type=F32)


def kernel(
    n, keep, scale,
    cols_ref, count_ref, feat_ref, w_ref, vals_hbm, cot_ref,
    act_ref, wg_ref, ig_ref,
    panel, vals, dense, acc, ys, yr, agg, pgr, gt, part, sibp, fresh, rsr,
    inv_v, inv_ref, wl, w1, s1, w2, wp, w3, w4, wo,
    vals_sem, inv_sem, ag_s, ag_r, sb_s, sb_r, so_s, so_r, y_s, y_r, g_s, g_r,
    sp_s, sp_r, rs_s, rs_r, wa_s, wa_r, wb_s, wb_r, wc_s, wc_r, wd_s, wd_r, we_s, we_r,
):
    half = n // 2
    slots = vals.shape[1] - 1
    cols = n * TB
    grp = lax.axis_index("grp")
    row = lax.axis_index("row")
    core = lax.rem(row, 2)
    q = lax.div(row, 2)
    odd = lax.rem(q, 2)
    p = (1 - odd) * lax.div(q, 2) + odd * (n - lax.div(q + 1, 2))

    def chip(offset):
        at = lax.rem(p + offset + n, n)
        back = lax.div(at, half)
        return (1 - back) * 2 * at + back * (2 * (n - at) - 1)

    def peer(chip_id):
        return (grp, chip_id * 2 + core)

    sibling = (grp, q * 2 + 1 - core)
    partner = (1 - grp, row)
    across = (1 - grp, q * 2 + 1 - core)

    def rcopy(src, dst, ss, rs, dev):
        return pltpu.make_async_remote_copy(
            src_ref=src, dst_ref=dst, send_sem=ss, recv_sem=rs,
            device_id=dev, device_id_type=MESH,
        )

    load = pltpu.make_async_copy(vals_hbm, vals.at[:, pl.ds(0, slots)], vals_sem)
    load.start()

    barrier = pltpu.get_barrier_semaphore()
    for dev in (peer(chip(1)), peer(chip(-1)), sibling, partner):
        pl.semaphore_signal(barrier, inc=1, device_id=dev, device_id_type=MESH)
    for h in range(2):
        panel[q, core * 2 + h] = feat_ref[pl.ds(h * 256, 256), :]
    for t in range(TB):
        vals[t, slots] = jnp.zeros((BS, BS), BF16)
    at_col = lax.broadcasted_iota(jnp.int32, (TB, cols), 1)
    at_row = lax.broadcasted_iota(jnp.int32, (TB, cols), 0)
    live = jnp.zeros((TB, cols), jnp.int32)
    for t in range(TB):
        live = jnp.where(at_row == t, count_ref[0, t], live)
    table = jnp.full((TB, cols), slots, jnp.int32)
    for k in range(slots):
        hit = (cols_ref[0, :, k : k + 1] == at_col) & (live > k)
        table = jnp.where(hit, k, table)
    inv_v[...] = table
    inv_copy = pltpu.make_async_copy(inv_v, inv_ref, inv_sem)
    inv_copy.start()
    pl.semaphore_wait(barrier, 4)

    step = {CW: 1, CCW: -1}

    def lane(d, i):
        return i % 2 if d == CW else 1 - i % 2

    def ag(d, i):
        src = panel.at[chip(-step[d] * (i // 2)), core * 2 + lane(d, i)]
        return rcopy(src, src, ag_s.at[d, i], ag_r.at[d, i], peer(chip(step[d])))

    def ag_in(d, i):
        src = panel.at[chip(-step[d] * (i // 2 + 1)), core * 2 + lane(d, i)]
        return rcopy(src, src, ag_s.at[d, i], ag_r.at[d, i], peer(chip(step[d])))

    def sib(d, i, c):
        src = panel.at[chip(-step[d] * (i // 2 + 1)), c * 2 + lane(d, i)]
        return rcopy(src, src, sb_s.at[d, i], sb_r.at[d, i], sibling)

    def sib_own(c):
        src = panel.at[q, pl.ds(c * 2, 2)]
        return rcopy(src, src, so_s, so_r, sibling)

    def where_dense(chip_id):
        return chip_id if keep else 0

    def build(chip_id):
        to = where_dense(chip_id)

        def rows(t, carry):
            for j in range(TB):
                k = inv_ref[t, chip_id * TB + j]
                dense[to, pl.ds(t * BS, BS), pl.ds(j * BS, BS)] = vals[t, k]
            return carry

        lax.fori_loop(0, TB, rows, 0)

    def forward(chip_id, first=False):
        build(chip_id)
        to = where_dense(chip_id)

        def rows(m, carry):
            at = pl.ds(pl.multiple_of(m * 256, 256), 256)
            v = dot(dense[to, at, :], panel[chip_id].reshape(4 * 256, 256))
            acc[at, :] = v if first else acc[at, :] + v
            return carry

        lax.fori_loop(0, 4, rows, 0)

    for i in range(2):
        for d in (CW, CCW):
            ag(d, i).start()
    sib_own(core).start()
    inv_copy.wait()
    load.wait()

    def arrive(i):
        for d in (CW, CCW):
            ag_in(d, i).wait_recv()
            if i + 2 < n - 1:
                ag(d, i + 2).start()
            sib(d, i, core).start()

    def sib_wait(dist, d):
        for i in (2 * dist - 2, 2 * dist - 1):
            sib(d, i, 1 - core).wait_recv()

    sib_own(1 - core).wait_recv()
    forward(q, True)
    for dist in range(1, half):
        arrive(2 * dist - 2)
        if dist > 1:
            sib_wait(dist - 1, CW)
            forward(chip(-(dist - 1)))
        arrive(2 * dist - 1)
        if dist > 1:
            sib_wait(dist - 1, CCW)
            forward(chip(dist - 1))
    for d in (CW, CCW):
        sib_wait(half - 1, d)
        forward(chip(-step[d] * (half - 1)))
    far = chip(half)
    build(far)
    arrive(n - 2)
    for d in (CW, CCW):
        sib(d, n - 2, 1 - core).wait_recv()

    at_far = where_dense(far)
    mine, theirs = grp * VD, (1 - grp) * VD

    def yc(k):
        return rcopy(ys.at[k], yr.at[k], y_s.at[k], y_r.at[k], partner)

    for k in range(4):
        at = pl.ds(pl.multiple_of(theirs + k * BS, BS), BS)
        v = acc[at, :] + dot(dense[at_far, at, :], panel[far].reshape(4 * 256, 256))
        ys[k] = v.astype(BF16)
        yc(k).start()
    for k in range(2):
        at = pl.ds(pl.multiple_of(mine + k * 256, 256), 256)
        acc[at, :] += dot(dense[at_far, at, :], panel[far].reshape(4 * 256, 256))

    def gc(k, base):
        ref = gt.at[:, pl.ds(pl.multiple_of(base + k * BS, BS), BS)]
        return rcopy(ref, ref, g_s.at[k], g_r.at[k], partner)

    for k in range(4):
        yc(k).wait_recv()
        here = pl.ds(k * BS, BS)
        at = pl.ds(pl.multiple_of(mine + k * BS, BS), BS)
        a = (acc[at, :] + yr[k].astype(F32)).astype(BF16)
        agg[here, :] = a
        pre = dot(a, w_ref[...])
        s = jax.nn.sigmoid(pre)
        act_ref[here, :] = (pre * s).astype(BF16)
        grad = (cot_ref[here, :].astype(F32) * (s * (1.0 + pre * (1.0 - s)))).astype(BF16)
        pgr[here, :] = grad
        back = lax.dot_general(
            w_ref[...], grad, (((1,), (1,)), ((), ())), preferred_element_type=F32
        )
        gt[:, at] = back.astype(BF16)
        gc(k, mine).start()
    local = lax.dot_general(
        agg[...], pgr[...], (((0,), (0,)), ((), ())), preferred_element_type=F32
    )
    for c in range(2):
        wl[c] = local[c * 128 : (c + 1) * 128]

    wa = lambda: rcopy(wl.at[1 - core], w1, wa_s, wa_r, sibling)
    wb = lambda: rcopy(s1.at[1 - grp], w2, wb_s, wb_r, partner)
    wc = lambda o: rcopy(wp.at[chip(o)], w3.at[q], wc_s.at[o], wc_r.at[o], peer(chip(o)))
    wd = lambda o: rcopy(w4.at[q], w4.at[q], wd_s.at[o], wd_r.at[o], peer(chip(o)))
    me_wo = core * 2 + grp
    outs = (sibling, partner, across)
    theirs_wo = ((1 - core) * 2 + grp, core * 2 + 1 - grp, (1 - core) * 2 + 1 - grp)
    we = lambda k: rcopy(wo.at[me_wo], wo.at[me_wo], we_s.at[k], we_r.at[k], outs[k])
    share = 64 // n

    def w_stage1():
        wa().wait_recv()
        total = wl[core] + w1[...]
        for k in range(2):
            s1[k] = total[k * 64 : (k + 1) * 64]
        wb().start()

    def w_stage2():
        wb().wait_recv()
        total = s1[grp] + w2[...]
        for k in range(n):
            wp[k] = total[k * share : (k + 1) * share]
        for o in range(1, n):
            wc(o).start()
        w3[q] = wp[q]

    def w_stage3():
        for o in range(1, n):
            rcopy(wp.at[q], w3.at[chip(-o)], wc_s.at[o], wc_r.at[o], peer(chip(o))).wait_recv()
        total = w3[0]
        for k in range(1, n):
            total = total + w3[k]
        w4[q] = total * scale
        for o in range(1, n):
            wd(o).start()

    def w_stage4():
        for o in range(1, n):
            there = w4.at[chip(-o)]
            rcopy(there, there, wd_s.at[o], wd_r.at[o], peer(chip(o))).wait_recv()
        for k in range(n):
            wo[me_wo, pl.ds(k * share, share), :] = w4[k]
        for k in range(3):
            we(k).start()

    def w_stage5():
        for k in range(3):
            there = wo.at[theirs_wo[k]]
            rcopy(there, there, we_s.at[k], we_r.at[k], outs[k]).wait_recv()
        for k in range(4):
            wg_ref[pl.ds(k * 64, 64), :] = wo[k]

    wa().start()
    for k in range(4):
        gc(k, theirs).wait_recv()

    def backward(chip_id):
        if not keep:
            build(chip_id)
        to = where_dense(chip_id)
        for j in range(4):
            v = dot(gt[...], dense[to, :, pl.ds(j * 256, 256)])
            part[chip_id, j] = v.astype(BF16)
        sp(chip_id).start()

    def sp(chip_id):
        return rcopy(
            part.at[chip_id, pl.ds((1 - core) * 2, 2)], sibp.at[chip_id],
            sp_s.at[chip_id], sp_r.at[chip_id], sibling,
        )

    def rs(d, i):
        src = rsr.at[d, i + 2] if i + 2 < n - 1 else fresh.at[d, i - (n - 3)]
        return rcopy(src, rsr.at[d, i], rs_s.at[d, i], rs_r.at[d, i], peer(chip(-step[d])))

    def summed(d, i):
        chip_id = chip(-step[d] * (i // 2 + 1))
        h = lane(d, i)
        own = part[chip_id, core * 2 + h].astype(F32) + sibp[chip_id, h].astype(F32)
        if i + 2 < n - 1:
            rs(d, i + 2).wait_recv()
            rsr[d, i + 2] = (own + rsr[d, i + 2].astype(F32)).astype(BF16)
        else:
            fresh[d, i - (n - 3)] = own.astype(BF16)
        rs(d, i).start()

    backward(far)
    backward(chip(-(half - 1)))
    sp(far).wait_recv()
    for d in (CW, CCW):
        summed(d, n - 2)
    w_stage1()
    backward(chip(half - 1))
    stages = [w_stage2, w_stage3, w_stage4]
    for dist in range(half - 1, 0, -1):
        for d in (CW, CCW):
            sp(chip(-step[d] * dist)).wait_recv()
            summed(d, 2 * dist - 1)
        if dist > 1:
            backward(chip(-(dist - 1)))
            backward(chip(dist - 1))
        else:
            backward(q)
        if stages:
            stages.pop(0)()
        for d in (CW, CCW):
            summed(d, 2 * dist - 2)
    for stage in stages:
        stage()
    sp(q).wait_recv()
    for h in range(2):
        total = part[q, core * 2 + h].astype(F32) + sibp[q, h].astype(F32)
        for d in (CW, CCW):
            i = h if d == CW else 1 - h
            rs(d, i).wait_recv()
            total = total + rsr[d, i].astype(F32)
        ig_ref[pl.ds(h * 256, 256), :] = total.T.astype(BF16)
    w_stage5()

    for d in (CW, CCW):
        for i in range(n - 1):
            ag(d, i).wait_send()
            sib(d, i, core).wait_send()
            rs(d, i).wait_send()
    sib_own(core).wait_send()
    for k in range(4):
        yc(k).wait_send()
        gc(k, mine).wait_send()
    for k in range(n):
        sp(k).wait_send()
    wa().wait_send()
    wb().wait_send()
    for o in range(1, n):
        wc(o).wait_send()
        wd(o).wait_send()
    for k in range(3):
        we(k).wait_send()


def hand_vm(a, b, c, x, y, z):
    x[...] = a[...]
    y[...] = b[...]
    z[...] = c[...]


def body(features, weight, block_vals, block_cols, block_count, cotangent):
    rows_dev, width = features.shape
    slots = block_vals.shape[2]
    groups = lax.axis_size("grp")
    members = lax.axis_size("row")
    verts = rows_dev * groups * members
    n = members // 2
    cols = members * rows_dev // BS
    keep = n <= 8
    dma, vm = pltpu.SemaphoreType.DMA, pltpu.VMEM
    share = 64 // n
    scratch = [
        vm((n, 4, 256, width), BF16),
        vm((TB, slots + 1, BS, BS), BF16),
        vm((n if keep else 1, 1024, 1024), BF16),
        vm((1024, width), F32),
        vm((4, BS, width), BF16),
        vm((4, BS, width), BF16),
        vm((rows_dev, width), BF16),
        vm((rows_dev, width), BF16),
        vm((width, 1024), BF16),
        vm((n, 4, width, 256), BF16),
        vm((n, 2, width, 256), BF16),
        vm((2, 2, width, 256), BF16),
        vm((2, n - 1, width, 256), BF16),
        vm((TB, cols), jnp.int32),
        pltpu.SMEM((TB, cols), jnp.int32),
        vm((2, 128, width), F32),
        vm((128, width), F32),
        vm((2, 64, width), F32),
        vm((64, width), F32),
        vm((n, share, width), F32),
        vm((n, share, width), F32),
        vm((n, share, width), F32),
        vm((4, 64, width), F32),
        dma, dma,
        dma((2, n - 1)), dma((2, n - 1)),
        dma((2, n - 1)), dma((2, n - 1)),
        dma, dma,
        dma((4,)), dma((4,)), dma((4,)), dma((4,)),
        dma((n,)), dma((n,)),
        dma((2, n - 1)), dma((2, n - 1)),
        dma, dma, dma, dma,
        dma((n,)), dma((n,)), dma((n,)), dma((n,)),
        dma((3,)), dma((3,)),
    ]
    whole = pl.BlockSpec(memory_space=pltpu.VMEM)
    results = pl.pallas_call(
        functools.partial(kernel, n, keep, 1.0 / math.sqrt(verts)),
        out_shape=(
            jax.ShapeDtypeStruct((rows_dev, width), BF16),
            jax.ShapeDtypeStruct((width, width), F32),
            jax.ShapeDtypeStruct((rows_dev, width), BF16),
        ),
        in_specs=[
            whole,
            pl.BlockSpec(memory_space=pltpu.SMEM),
            whole,
            whole,
            pl.BlockSpec(memory_space=pl.ANY),
            whole,
        ],
        out_specs=(whole, whole, whole),
        scratch_shapes=scratch,
        compiler_params=pltpu.CompilerParams(
            collective_id=0, has_side_effects=True, vmem_limit_bytes=60 * 1024 * 1024
        ),
    )(block_cols, block_count, features, weight, block_vals[0], cotangent)
    return pl.pallas_call(
        hand_vm,
        out_shape=tuple(jax.ShapeDtypeStruct(r.shape, r.dtype) for r in results),
    )(*results)


def solution(mesh):
    placed = (
        P(("grp", "row"), None),
        P(),
        P("grp", "row", None, None, None),
        P("grp", "row", None),
        P("grp", "row"),
        P(("grp", "row"), None),
    )
    return jax.shard_map(
        body,
        mesh=mesh,
        in_specs=placed,
        out_specs=(P(("grp", "row"), None), P(), P(("grp", "row"), None)),
        check_vma=False,
    )
```
